32 devices in a mesh: dp: 4 (over y, core), expert: 8 (over z, x).
Axes of the slice: x: 2, y: 2, z: 4, core: 2. Of those that a mesh axis runs over, the one named last changes fastest.
Arguments:
- tokens: bfloat16 [4096, 1024], P(('dp', 'expert')), may hold values from -6 to 6
- expert_ids: int32 [4096, 8], P(('dp', 'expert')), may hold values from 0 to 31, as said below
- route_num: int32 [4096, 8], P(('dp', 'expert')), may hold values from 1 to 256
- w_gate: bfloat16 [32, 1024, 384], P('expert'), may hold values from -0.1875 to 0.1875
- w_up: bfloat16 [32, 1024, 384], P('expert'), may hold values from -0.1875 to 0.1875
- w_down: bfloat16 [32, 384, 1024], P('expert'), may hold values from -0.3125 to 0.3125
- cotangent: bfloat16 [4096, 1024], P(('dp', 'expert')), may hold values from -1.1953125 to 1.1953125
Outputs:
- output: bfloat16 [4096, 1024], P(('dp', 'expert'))
- tokens_grad: bfloat16 [4096, 1024], P(('dp', 'expert'))
- w_gate_grad: bfloat16 [32, 1024, 384], P('expert', 'dp')
- w_up_grad: bfloat16 [32, 1024, 384], P('expert', 'dp')
- w_down_grad: bfloat16 [32, 384, 1024], P('expert', None, 'dp')
The draws below stay inside these ranges and needn't reach their ends.
Inputs may be any that keep to these rules, and one draw needn't show every extreme that they name: `expert_ids`: each row names 8 different experts. Rows come in aligned blocks of 128, one device's tokens each, and 8 consecutive blocks form one data group. In each data group one expert is named by exactly 40 rows of every block of that group, and in no block is any expert named by more than 40 rows.
All inputs are finite; a program needn't handle non-finite values.
Results may differ from the reference program's by a relative error of at most 0.017.
Values may be sent and summed in bfloat16 or wider, within the bound.
A program may use at most 128 MiB of HBM per device.

```python
import jax
import jax.numpy as jnp
from jax import lax

D = 1024
FF = 384
TOP = 8
DENOM = 256
TOK_DEV = 128
CAP = 40
RANKS = 8
EXPERTS = 32
TOKENS = 4096


def draw_expert_ids(key, part):
    key = jax.random.fold_in(key, 11)
    block_count = TOKENS // TOK_DEV
    other_picks = TOK_DEV * TOP - CAP
    span_low = max(2 * TOP, (other_picks + CAP - 1) // CAP)

    def one_block(block_idx):
        group_idx = block_idx // RANKS
        group_key = jax.random.fold_in(jax.random.fold_in(key, 7), group_idx)
        block_key = jax.random.fold_in(key, block_idx)
        hot_expert = jax.random.randint(group_key, (), 0, EXPERTS)
        key_order, key_rows, key_span, key_turn = jax.random.split(block_key, 4)
        row_order = jax.random.permutation(key_order, TOK_DEV)
        hot_row = (row_order < CAP).astype(jnp.int32)
        other_experts = jax.random.permutation(key_rows, EXPERTS - 1)
        other_experts = jnp.where(other_experts >= hot_expert, other_experts + 1, other_experts)
        span_len = jax.random.randint(key_span, (), span_low, EXPERTS)
        need_count = TOP - hot_row
        start_pos = jnp.cumsum(need_count) - need_count
        slot_pos = jnp.arange(TOP, dtype=jnp.int32)
        cycle_pos = jnp.mod(start_pos[:, None] + slot_pos[None, :] - hot_row[:, None], span_len)
        chosen = other_experts[cycle_pos]
        chosen = jnp.where((hot_row[:, None] == 1) & (slot_pos[None, :] == 0), hot_expert, chosen)
        rotation = jax.random.randint(key_turn, (TOK_DEV, 1), 0, TOP)
        columns = jnp.mod(slot_pos[None, :] + rotation, TOP)
        return jnp.take_along_axis(chosen, columns, axis=1)
    expert_table = jax.vmap(one_block)(jnp.arange(block_count, dtype=jnp.int32))
    return expert_table.reshape(TOKENS, TOP).astype(jnp.int32)


def touch_ends(array, stream_key, least, high):
    place = [jax.random.randint(jax.random.fold_in(stream_key, axis), (), 0, length) for axis, length in enumerate(array.shape)]
    longest = array.shape.index(max(array.shape))
    next_to = place[:longest] + [(place[longest] + 1) % array.shape[longest]] + place[longest + 1:]
    return array.at[tuple(place)].set(least).at[tuple(next_to)].set(high)


def shard_levels(stream_key, extent, cuts, smallest, top_value):
    factor_of = 1.0
    for dim, blocks in cuts:
        draws = jax.random.uniform(jax.random.fold_in(jax.random.fold_in(stream_key, 6), dim), (blocks,), jnp.float32, smallest / len(cuts), top_value / len(cuts))
        factor_of = factor_of * jnp.repeat(jnp.exp(draws), extent[dim] // blocks).reshape((-1,) + (1,) * (len(extent) - 1 - dim))
    return factor_of


def centred(stream_key, extent, spread, bound, cuts=(), kind=jnp.bfloat16):
    result = spread * jax.random.normal(stream_key, extent, jnp.float32)
    if cuts:
        result = result * shard_levels(stream_key, extent, cuts, -0.22, 0.18)
    return jnp.clip(result, -bound, bound).astype(kind)


def setup_inputs(seed: int = 0) -> dict:
    splits = jax.random.split(jax.random.key(seed), 8)
    tokens = centred(splits[0], (TOKENS, D), 1.0, 6.0, ((0, 32),))
    expert_ids = draw_expert_ids(jax.random.fold_in(splits[7], 71), 0)
    route_num = touch_ends(jax.random.randint(splits[2], (TOKENS, TOP), 1, DENOM + 1), jax.random.fold_in(splits[2], 1), 1, DENOM).astype(jnp.int32)
    w_gate = centred(splits[3], (EXPERTS, D, FF), D ** -0.5, 0.1875, ((0, 8),))
    w_up = centred(splits[4], (EXPERTS, D, FF), D ** -0.5, 0.1875, ((0, 8),))
    w_down = centred(splits[5], (EXPERTS, FF, D), FF ** -0.5, 0.3125, ((0, 8),))
    cotangent = centred(splits[6], (TOKENS, D), 0.2, 1.1953125, ((0, 32),))
    return {"tokens": tokens, "expert_ids": expert_ids, "route_num": route_num, "w_gate": w_gate, "w_up": w_up, "w_down": w_down, "cotangent": cotangent}


def rounded(value):
    return lax.optimization_barrier(value.astype(jnp.bfloat16)).astype(jnp.float32)


def group_sum(parts):
    return jnp.sum(parts.astype(jnp.float32), axis=0).astype(jnp.bfloat16)


def reference(tokens, expert_ids, route_num, w_gate, w_up, w_down, cotangent):
    highest = lax.Precision.HIGHEST
    group_tok = TOK_DEV * RANKS
    group_picks = group_tok * TOP
    rows_max = RANKS * CAP
    all_picks = TOKENS * TOP
    group_count = TOKENS // group_tok
    flat_ids = expert_ids.reshape(all_picks)
    route_weight = route_num.astype(jnp.float32) / DENOM
    flat_weight = route_weight.reshape(all_picks)

    def expert_group(expert, group, gate_w, up_w, down_w):
        first = (group * group_picks).astype(jnp.int32)
        chosen = lax.dynamic_slice_in_dim(flat_ids, first, group_picks)
        marked = (chosen == expert).astype(jnp.int32)
        order = (jnp.cumsum(marked) - 1).astype(jnp.int32)
        target = jnp.where(marked == 1, order, rows_max).astype(jnp.int32)
        local_pick = jnp.full((rows_max + 1,), group_picks, jnp.int32)
        local_pick = local_pick.at[target].set(jnp.arange(group_picks, dtype=jnp.int32))[:rows_max]
        filled = local_pick < group_picks
        pick_at = jnp.where(filled, first + local_pick, all_picks).astype(jnp.int32)
        safe_pick = jnp.minimum(pick_at, all_picks - 1).astype(jnp.int32)
        token_at = (safe_pick // TOP).astype(jnp.int32)
        weight_at = jnp.where(filled, flat_weight[safe_pick], jnp.float32(0.0))
        x_rows = jnp.where(filled[:, None], tokens[token_at].astype(jnp.float32), jnp.float32(0.0))
        grad_rows = rounded(weight_at[:, None] * cotangent[token_at].astype(jnp.float32))
        pre_gate = jnp.dot(x_rows, gate_w, precision=highest)
        pre_up = jnp.dot(x_rows, up_w, precision=highest)
        sigmoid_gate = jax.nn.sigmoid(pre_gate)
        activation = pre_gate * sigmoid_gate
        hidden = rounded(activation * pre_up)
        out_rows = jnp.dot(hidden, down_w, precision=highest).astype(jnp.bfloat16)
        hidden_grad = jnp.dot(grad_rows, down_w.T, precision=highest)
        gate_grad = rounded(hidden_grad * pre_up * sigmoid_gate * (1.0 + pre_gate * (1.0 - sigmoid_gate)))
        up_grad = rounded(hidden_grad * activation)
        pick_grad = (jnp.dot(gate_grad, gate_w.T, precision=highest) + jnp.dot(up_grad, up_w.T, precision=highest)).astype(jnp.bfloat16)
        gate_part = jnp.dot(x_rows.T, gate_grad, precision=highest).astype(jnp.bfloat16)
        up_part = jnp.dot(x_rows.T, up_grad, precision=highest).astype(jnp.bfloat16)
        down_part = jnp.dot(hidden.T, grad_rows, precision=highest).astype(jnp.bfloat16)
        return out_rows, pick_grad, pick_at, gate_part, up_part, down_part

    def expert_step(carry, expert):
        out_all, grad_all = carry
        gate_w = w_gate[expert].astype(jnp.float32)
        up_w = w_up[expert].astype(jnp.float32)
        down_w = w_down[expert].astype(jnp.float32)

        def one_group(group):
            return expert_group(expert, group, gate_w, up_w, down_w)

        out_rows, pick_grad, pick_at, gate_part, up_part, down_part = lax.map(one_group, jnp.arange(group_count, dtype=jnp.int32))
        flat_at = pick_at.reshape(-1)
        out_all = out_all.at[flat_at].set(out_rows.reshape(-1, D))
        grad_all = grad_all.at[flat_at].set(pick_grad.reshape(-1, D))
        return (out_all, grad_all), (group_sum(gate_part), group_sum(up_part), group_sum(down_part))

    start_rows = jnp.zeros((all_picks + 1, D), jnp.bfloat16)
    (out_all, grad_all), (gate_total, up_total, down_total) = lax.scan(expert_step, (start_rows, start_rows), jnp.arange(EXPERTS, dtype=jnp.int32))
    out_picks = out_all[:all_picks].reshape(TOKENS, TOP, D)
    grad_picks = grad_all[:all_picks].reshape(TOKENS, TOP, D)
    out_sum = jnp.zeros((TOKENS, D), jnp.float32)
    grad_sum = jnp.zeros((TOKENS, D), jnp.float32)
    for slot_k in range(TOP):
        out_sum = out_sum + route_weight[:, slot_k, None] * out_picks[:, slot_k].astype(jnp.float32)
        grad_sum = grad_sum + grad_picks[:, slot_k].astype(jnp.float32)
    return (out_sum.astype(jnp.bfloat16), grad_sum.astype(jnp.bfloat16), gate_total, up_total, down_total)
```

```python
import jax
import jax.numpy as jnp
from jax import lax
from jax.sharding import PartitionSpec as P

DENOM = 256


def local(tokens, expert_ids, route_num, w_gate, w_up, w_down, cotangent):
    exp_dev = w_gate.shape[0]
    width = tokens.shape[1]
    ranks = lax.axis_size("expert")
    rows = tokens.shape[0]
    capacity = 5 * rows // 16
    bf16, f32 = jnp.bfloat16, jnp.float32

    packed = lax.all_gather(expert_ids * 512 + route_num, "expert")
    x_all = lax.all_gather(tokens, "expert")
    c_all = lax.all_gather(cotangent, "expert")

    ids, num = packed // 512, packed % 512
    first = lax.axis_index("expert") * exp_dev
    mine = first + jnp.arange(exp_dev, dtype=jnp.int32)
    named = ids[:, :, :, None] == mine
    match = jnp.any(named, axis=2)
    weight = jnp.sum(jnp.where(named, num[..., None], 0), axis=2).astype(f32) / DENOM
    earlier = jnp.tril(jnp.ones((rows, rows), bf16), -1)
    rank = jnp.einsum("ut,bte->beu", earlier, match.astype(bf16), preferred_element_type=f32)
    slot = jnp.where(match.transpose(0, 2, 1), rank.astype(jnp.int32), -1)
    place = slot[:, :, None, :] == jnp.arange(capacity, dtype=jnp.int32)[:, None]
    pick = place.astype(bf16)
    pick_w = jnp.where(place, weight.transpose(0, 2, 1)[:, :, None, :], 0.0).astype(bf16)
    pick = pick.reshape(ranks, exp_dev * capacity, rows)
    pick_w = pick_w.reshape(ranks, exp_dev * capacity, rows)

    def to_slots(sel, vals):
        got = jnp.einsum("bst,btd->bsd", sel, vals, preferred_element_type=f32).astype(bf16)
        got = got.reshape(ranks, exp_dev, capacity, width).transpose(1, 0, 2, 3)
        return got.reshape(exp_dev, ranks * capacity, width)

    def from_slots(sel, vals):
        vals = vals.reshape(exp_dev, ranks, capacity, width).transpose(1, 0, 2, 3)
        vals = vals.reshape(ranks, exp_dev * capacity, width)
        part = jnp.einsum("bst,bsd->btd", sel, vals, preferred_element_type=f32).astype(bf16)
        return lax.psum_scatter(part.reshape(ranks * rows, width), "expert", scatter_dimension=0, tiled=True)

    x_rows = to_slots(pick, x_all)
    pre_gate = jnp.einsum("erd,edf->erf", x_rows, w_gate, preferred_element_type=f32)
    pre_up = jnp.einsum("erd,edf->erf", x_rows, w_up, preferred_element_type=f32)
    sig = jax.nn.sigmoid(pre_gate)
    act = pre_gate * sig
    hidden = (act * pre_up).astype(bf16)
    expert_out = jnp.einsum("erf,efd->erd", hidden, w_down, preferred_element_type=f32).astype(bf16)
    output = from_slots(pick_w, expert_out)
    do_rows = to_slots(pick_w, c_all)
    hidden_grad = jnp.einsum("erd,efd->erf", do_rows, w_down, preferred_element_type=f32)
    gate_grad = (hidden_grad * pre_up * sig * (1.0 + pre_gate * (1.0 - sig))).astype(bf16)
    up_grad = (hidden_grad * act).astype(bf16)
    pick_grad = (
        jnp.einsum("erf,edf->erd", gate_grad, w_gate, preferred_element_type=f32)
        + jnp.einsum("erf,edf->erd", up_grad, w_up, preferred_element_type=f32)
    ).astype(bf16)
    tokens_grad = from_slots(pick, pick_grad)
    down_part = jnp.einsum("erf,erd->efd", hidden, do_rows, preferred_element_type=f32)
    gate_part = jnp.einsum("erd,erf->edf", x_rows, gate_grad, preferred_element_type=f32)
    up_part = jnp.einsum("erd,erf->edf", x_rows, up_grad, preferred_element_type=f32)
    down_total = lax.psum_scatter(down_part.astype(bf16), "dp", scatter_dimension=2, tiled=True)
    gate_total = lax.psum_scatter(gate_part.astype(bf16), "dp", scatter_dimension=1, tiled=True)
    up_total = lax.psum_scatter(up_part.astype(bf16), "dp", scatter_dimension=1, tiled=True)
    return output, tokens_grad, gate_total, up_total, down_total


def solution(mesh):
    in_specs = (
        P(("dp", "expert"), None),
        P(("dp", "expert"), None),
        P(("dp", "expert"), None),
        P("expert", None, None),
        P("expert", None, None),
        P("expert", None, None),
        P(("dp", "expert"), None),
    )
    out_specs = (
        P(("dp", "expert"), None),
        P(("dp", "expert"), None),
        P("expert", "dp", None),
        P("expert", "dp", None),
        P("expert", None, "dp"),
    )
    return jax.shard_map(local, mesh=mesh, in_specs=in_specs, out_specs=out_specs, check_vma=False)
```

```python
import functools

import jax
import jax.numpy as jnp
from jax import lax
from jax.experimental import pallas as pl
from jax.experimental.pallas import tpu as pltpu
from jax.sharding import PartitionSpec as P

DENOM = 256
MESH = pl.DeviceIdType.MESH
ANY = pl.BlockSpec(memory_space=pl.ANY)
VMEM = pl.BlockSpec(memory_space=pltpu.VMEM)


def greet(axes):
    barrier = pltpu.get_barrier_semaphore()
    count = 0
    for axis, size in axes:
        major, minor, groups = split_index(axis, size)
        peers = [2 * major + 1 - minor]
        peers += [2 * lax.rem(major + k, groups) + minor for k in range(1, groups)]
        for peer in peers:
            pl.semaphore_signal(barrier, inc=1, device_id={axis: peer}, device_id_type=MESH)
        count += len(peers)
    pl.semaphore_wait(barrier, count)


def split_index(axis, size):
    me = lax.axis_index(axis)
    return me // 2, lax.rem(me, 2), size // 2


def gather_kernel(ranks, *refs):
    srcs, outs, (send, recv, local_sem) = refs[:3], refs[3:6], refs[6:]
    major, minor, groups = split_index("expert", ranks)
    me = 2 * major + minor
    partner = 2 * major + 1 - minor
    greet([("expert", ranks)])
    copies = []

    def push(t, src, shard, slot, peer):
        copy = pltpu.make_async_remote_copy(
            src_ref=src, dst_ref=outs[t].at[shard], send_sem=send.at[t, slot], recv_sem=recv.at[t, shard],
            device_id={"expert": peer}, device_id_type=MESH,
        )
        copy.start()
        copies.append(copy)

    def arrived(t, shard):
        pltpu.make_async_remote_copy(
            src_ref=outs[t].at[shard], dst_ref=outs[t].at[shard], send_sem=send.at[t, 0], recv_sem=recv.at[t, shard],
            device_id={"expert": partner}, device_id_type=MESH,
        ).wait_recv()

    for t in range(3):
        push(t, srcs[t], me, 0, partner)
        for k in range(1, groups):
            push(t, srcs[t], me, k, 2 * lax.rem(major + k, groups) + minor)
    keep = [pltpu.make_async_copy(srcs[t], outs[t].at[me], local_sem.at[t]) for t in range(3)]
    for copy in keep:
        copy.start()
    for t in range(3):
        for k in range(1, groups):
            shard = 2 * lax.rem(major - k + groups, groups) + minor
            arrived(t, shard)
            push(t, outs[t].at[shard], shard, groups + k - 1, partner)
    for t in range(3):
        for k in range(groups):
            arrived(t, 2 * lax.rem(major - k + groups, groups) + 1 - minor)
    for copy in copies:
        copy.wait_send()
    for copy in keep:
        copy.wait()


def gather(ranks, packed, tokens, cotangent):
    srcs = (packed, tokens, cotangent)
    return pl.pallas_call(
        functools.partial(gather_kernel, ranks),
        out_shape=[jax.ShapeDtypeStruct((ranks, *a.shape), a.dtype) for a in srcs],
        in_specs=[ANY] * 3,
        out_specs=[ANY] * 3,
        scratch_shapes=[
            pltpu.SemaphoreType.DMA((3, ranks)),
            pltpu.SemaphoreType.DMA((3, ranks)),
            pltpu.SemaphoreType.DMA((3,)),
        ],
        compiler_params=pltpu.CompilerParams(collective_id=0, has_side_effects=True),
    )(*srcs)


class Job:
    def __init__(self, axis, size, source, land, stage, got, sems):
        self.axis, self.source, self.land, self.stage, self.got = axis, source, land, stage, got
        self.s1, self.r1, self.s2, self.r2, self.ls = sems
        self.major, self.minor, self.groups = split_index(axis, size)
        self.partner = 2 * self.major + 1 - self.minor
        self.copies = []

    def remote(self, src, dst, s, r, peer):
        return pltpu.make_async_remote_copy(
            src_ref=src, dst_ref=dst, send_sem=s, recv_sem=r, device_id={self.axis: peer}, device_id_type=MESH
        )

    def target(self, k):
        return lax.rem(self.major + k, self.groups)

    def order(self):
        return list(range(1, self.groups)) + [0]

    def exchange(self):
        for k in self.order():
            to = self.target(k)
            copy = self.remote(
                self.source(2 * to + 1 - self.minor), self.land.at[k], self.s1.at[k], self.r1.at[k], self.partner
            )
            copy.start()
            self.copies.append(copy)
            pltpu.make_async_copy(self.source(2 * to + self.minor), self.stage.at[k], self.ls.at[k]).start()

    def pair_sum(self, k):
        pltpu.make_async_copy(self.source(2 * self.target(k) + self.minor), self.stage.at[k], self.ls.at[k]).wait()
        self.remote(self.land.at[k], self.land.at[k], self.s1.at[k], self.r1.at[k], self.partner).wait_recv()
        total = self.stage[k].astype(jnp.float32) + self.land[k].astype(jnp.float32)
        self.stage[k] = total.astype(jnp.bfloat16)
        if k:
            copy = self.remote(
                self.stage.at[k], self.got.at[k - 1], self.s2.at[k - 1], self.r2.at[k - 1],
                2 * self.target(k) + self.minor,
            )
            copy.start()
            self.copies.append(copy)

    def finish(self):
        total = self.stage[0].astype(jnp.float32)
        for k in range(1, self.groups):
            slot = self.got.at[k - 1]
            self.remote(slot, slot, self.s2.at[k - 1], self.r2.at[k - 1], self.partner).wait_recv()
            total = total + self.got[k - 1].astype(jnp.float32)
        return total.astype(jnp.bfloat16)

    def drain(self):
        for copy in self.copies:
            copy.wait_send()


def reduce_kernel(ranks, groups_dp, exp_dev, *refs):
    (part_o, part_t, part_g, part_u, part_d), refs = refs[:5], refs[5:]
    (out_o, out_t, out_g, out_u, out_d), refs = refs[:5], refs[5:]
    (land_e, stage_e, got_e, land_w, stage_w, got_w, land_d, stage_d, got_d), refs = refs[:9], refs[9:]
    sems_e, sems_w = refs[:5], refs[5:10]
    span = out_g.shape[1]
    greet([("expert", ranks), ("dp", groups_dp)])
    tok_jobs = [
        Job("expert", ranks, lambda i, p=p: p.at[i], land_e.at[j], stage_e.at[j], got_e.at[j], [s.at[j] for s in sems_e])
        for j, p in enumerate((part_o, part_t))
    ]
    w_jobs = []
    for e in range(exp_dev):
        for j, p in enumerate((part_g, part_u)):
            w_jobs.append(Job(
                "dp", groups_dp, lambda i, p=p, e=e: p.at[e, pl.ds(pl.multiple_of(i * span, span), span), :],
                land_w.at[j, e], stage_w.at[j, e], got_w.at[j, e], [s.at[j, e] for s in sems_w],
            ))
        w_jobs.append(Job(
            "dp", groups_dp, lambda i, e=e: part_d.at[e, :, pl.ds(pl.multiple_of(i * span, span), span)],
            land_d.at[e], stage_d.at[e], got_d.at[e], [s.at[2, e] for s in sems_w],
        ))
    for job in tok_jobs + w_jobs:
        job.exchange()
    todo_t = [(job, k) for job in tok_jobs for k in job.order()]
    todo_w = [(job, k) for k in w_jobs[0].order() for job in w_jobs]
    while todo_t or todo_w:
        for todo in (todo_w, todo_t):
            if todo:
                job, k = todo.pop(0)
                job.pair_sum(k)
    out_o[...] = tok_jobs[0].finish()
    out_t[...] = tok_jobs[1].finish()
    for n, job in enumerate(w_jobs):
        (out_g, out_u, out_d)[n % 3][n // 3] = job.finish()
    for job in tok_jobs + w_jobs:
        job.drain()


def reduce_all(ranks, groups_dp, part_o, part_t, part_g, part_u, part_d):
    bf16 = jnp.bfloat16
    exp_dev, width, hid = part_g.shape
    rows = part_o.shape[1]
    span = width // groups_dp
    m_e, m_d = ranks // 2, groups_dp // 2

    def slots(lead, block, groups):
        return [
            pltpu.VMEM((*lead, groups, *block), bf16),
            pltpu.VMEM((*lead, groups, *block), bf16),
            pltpu.VMEM((*lead, groups - 1, *block), bf16),
        ]

    def sems(lead, groups):
        return [pltpu.SemaphoreType.DMA((*lead, groups)) for _ in range(5)]

    return pl.pallas_call(
        functools.partial(reduce_kernel, ranks, groups_dp, exp_dev),
        out_shape=[
            jax.ShapeDtypeStruct((rows, width), bf16),
            jax.ShapeDtypeStruct((rows, width), bf16),
            jax.ShapeDtypeStruct((exp_dev, span, hid), bf16),
            jax.ShapeDtypeStruct((exp_dev, span, hid), bf16),
            jax.ShapeDtypeStruct((exp_dev, hid, span), bf16),
        ],
        in_specs=[ANY] * 5,
        out_specs=[VMEM] * 5,
        scratch_shapes=[
            *slots((2,), (rows, width), m_e),
            *slots((2, exp_dev), (span, hid), m_d),
            *slots((exp_dev,), (hid, span), m_d),
            *sems((2,), m_e),
            *sems((3, exp_dev), m_d),
        ],
        compiler_params=pltpu.CompilerParams(
            collective_id=1, has_side_effects=True, vmem_limit_bytes=56 * 1024 * 1024
        ),
    )(part_o, part_t, part_g, part_u, part_d)


def local(tokens, expert_ids, route_num, w_gate, w_up, w_down, cotangent):
    exp_dev = w_gate.shape[0]
    width = tokens.shape[1]
    ranks = lax.axis_size("expert")
    rows = tokens.shape[0]
    capacity = 5 * rows // 16
    bf16, f32 = jnp.bfloat16, jnp.float32

    packed, x_all, c_all = gather(ranks, (expert_ids * 512 + route_num).T, tokens, cotangent)
    packed = packed.transpose(0, 2, 1)

    ids, num = packed // 512, packed % 512
    first = lax.axis_index("expert") * exp_dev
    mine = first + jnp.arange(exp_dev, dtype=jnp.int32)
    named = ids[:, :, :, None] == mine
    match = jnp.any(named, axis=2)
    weight = jnp.sum(jnp.where(named, num[..., None], 0), axis=2).astype(f32) / DENOM
    earlier = jnp.tril(jnp.ones((rows, rows), bf16), -1)
    rank = jnp.einsum("ut,bte->beu", earlier, match.astype(bf16), preferred_element_type=f32)
    slot = jnp.where(match.transpose(0, 2, 1), rank.astype(jnp.int32), -1)
    place = slot[:, :, None, :] == jnp.arange(capacity, dtype=jnp.int32)[:, None]
    pick = place.astype(bf16)
    pick_w = jnp.where(place, weight.transpose(0, 2, 1)[:, :, None, :], 0.0).astype(bf16)
    pick = pick.reshape(ranks, exp_dev * capacity, rows)
    pick_w = pick_w.reshape(ranks, exp_dev * capacity, rows)

    def to_slots(sel, vals):
        got = jnp.einsum("bst,btd->bsd", sel, vals, preferred_element_type=f32).astype(bf16)
        got = got.reshape(ranks, exp_dev, capacity, width).transpose(1, 0, 2, 3)
        return got.reshape(exp_dev, ranks * capacity, width)

    def from_slots(sel, vals):
        vals = vals.reshape(exp_dev, ranks, capacity, width).transpose(1, 0, 2, 3)
        vals = vals.reshape(ranks, exp_dev * capacity, width)
        part = jnp.einsum("bst,bsd->btd", sel, vals, preferred_element_type=f32).astype(bf16)
        return part

    x_rows = to_slots(pick, x_all)
    pre_gate = jnp.einsum("erd,edf->erf", x_rows, w_gate, preferred_element_type=f32)
    pre_up = jnp.einsum("erd,edf->erf", x_rows, w_up, preferred_element_type=f32)
    sig = jax.nn.sigmoid(pre_gate)
    act = pre_gate * sig
    hidden = (act * pre_up).astype(bf16)
    expert_out = jnp.einsum("erf,efd->erd", hidden, w_down, preferred_element_type=f32).astype(bf16)
    out_part = from_slots(pick_w, expert_out)
    do_rows = to_slots(pick_w, c_all)
    hidden_grad = jnp.einsum("erd,efd->erf", do_rows, w_down, preferred_element_type=f32)
    gate_grad = (hidden_grad * pre_up * sig * (1.0 + pre_gate * (1.0 - sig))).astype(bf16)
    up_grad = (hidden_grad * act).astype(bf16)
    pick_grad = (
        jnp.einsum("erf,edf->erd", gate_grad, w_gate, preferred_element_type=f32)
        + jnp.einsum("erf,edf->erd", up_grad, w_up, preferred_element_type=f32)
    ).astype(bf16)
    grad_part = from_slots(pick, pick_grad)
    down_part = jnp.einsum("erf,erd->efd", hidden, do_rows, preferred_element_type=f32)
    gate_part = jnp.einsum("erd,erf->edf", x_rows, gate_grad, preferred_element_type=f32)
    up_part = jnp.einsum("erd,erf->edf", x_rows, up_grad, preferred_element_type=f32)
    return tuple(reduce_all(
        ranks, lax.axis_size("dp"), out_part, grad_part,
        gate_part.astype(bf16), up_part.astype(bf16), down_part.astype(bf16),
    ))


def solution(mesh):
    in_specs = (
        P(("dp", "expert"), None),
        P(("dp", "expert"), None),
        P(("dp", "expert"), None),
        P("expert", None, None),
        P("expert", None, None),
        P("expert", None, None),
        P(("dp", "expert"), None),
    )
    out_specs = (
        P(("dp", "expert"), None),
        P(("dp", "expert"), None),
        P("expert", "dp", None),
        P("expert", "dp", None),
        P("expert", None, "dp"),
    )
    return jax.shard_map(local, mesh=mesh, in_specs=in_specs, out_specs=out_specs, check_vma=False)
```

```python
import functools

import jax
import jax.numpy as jnp
from jax import lax
from jax.experimental import pallas as pl
from jax.experimental.pallas import tpu as pltpu
from jax.sharding import PartitionSpec as P

DENOM = 256
MESH = pl.DeviceIdType.MESH
ANY = pl.BlockSpec(memory_space=pl.ANY)
VMEM = pl.BlockSpec(memory_space=pltpu.VMEM)
BF16, F32 = jnp.bfloat16, jnp.float32


def split_index(axis, size):
    me = lax.axis_index(axis)
    return me // 2, lax.rem(me, 2), size // 2


def greet(axes):
    barrier = pltpu.get_barrier_semaphore()
    count = 0
    for axis, size in axes:
        major, minor, groups = split_index(axis, size)
        peers = [2 * major + 1 - minor]
        peers += [2 * lax.rem(major + k, groups) + minor for k in range(1, groups)]
        for peer in peers:
            pl.semaphore_signal(barrier, inc=1, device_id={axis: peer}, device_id_type=MESH)
        count += len(peers)
    pl.semaphore_wait(barrier, count)


def dot(a, b, ca, cb):
    return lax.dot_general(a, b, (((ca,), (cb,)), ((), ())), preferred_element_type=F32)


class Gather:
    def __init__(self, ranks, src, out, send, recv, local_sem):
        self.src, self.out, self.send, self.recv = src, out, send, recv
        self.major, self.minor, self.groups = split_index("expert", ranks)
        self.me = 2 * self.major + self.minor
        self.partner = 2 * self.major + 1 - self.minor
        self.copies = []
        self.keep = pltpu.make_async_copy(src, out.at[self.me], local_sem)

    def push(self, src, shard, slot, peer):
        copy = pltpu.make_async_remote_copy(
            src_ref=src, dst_ref=self.out.at[shard], send_sem=self.send.at[slot], recv_sem=self.recv.at[shard],
            device_id={"expert": peer}, device_id_type=MESH,
        )
        copy.start()
        self.copies.append(copy)

    def arrived(self, shard):
        pltpu.make_async_remote_copy(
            src_ref=self.out.at[shard], dst_ref=self.out.at[shard], send_sem=self.send.at[0],
            recv_sem=self.recv.at[shard], device_id={"expert": self.partner}, device_id_type=MESH,
        ).wait_recv()

    def start(self):
        self.keep.start()
        self.push(self.src, self.me, 0, self.partner)
        for k in range(1, self.groups):
            self.push(self.src, self.me, k, 2 * lax.rem(self.major + k, self.groups) + self.minor)

    def forward(self, k):
        shard = 2 * lax.rem(self.major - k + self.groups, self.groups) + self.minor
        self.arrived(shard)
        self.push(self.out.at[shard], shard, self.groups + k - 1, self.partner)

    def finish(self):
        for k in range(self.groups):
            self.arrived(2 * lax.rem(self.major - k + self.groups, self.groups) + 1 - self.minor)
        self.keep.wait()

    def drain(self):
        for copy in self.copies:
            copy.wait_send()


class Job:
    def __init__(self, axis, size, source, land, got, sems, window):
        self.axis, self.source, self.land, self.got, self.window = axis, source, land, got, window
        self.s1, self.r1, self.s2, self.r2 = sems
        self.major, self.minor, self.groups = split_index(axis, size)
        self.partner = 2 * self.major + 1 - self.minor
        self.copies = []
        self.unsent = list(range(1, self.groups)) + [0]
        self.unsummed = list(self.unsent)

    def remote(self, src, dst, s, r, peer):
        return pltpu.make_async_remote_copy(
            src_ref=src, dst_ref=dst, send_sem=s, recv_sem=r, device_id={self.axis: peer}, device_id_type=MESH
        )

    def target(self, k):
        return lax.rem(self.major + k, self.groups)

    def own(self, k):
        return self.source.at[2 * self.target(k) + self.minor]

    def send_next(self):
        if self.unsent:
            k = self.unsent.pop(0)
            copy = self.remote(
                self.source.at[2 * self.target(k) + 1 - self.minor], self.land.at[k], self.s1.at[k], self.r1.at[k],
                self.partner,
            )
            copy.start()
            self.copies.append(copy)

    def exchange(self):
        for _ in range(self.window):
            self.send_next()

    def sum_next(self):
        if not self.unsummed:
            return
        k = self.unsummed.pop(0)
        self.remote(self.land.at[k], self.land.at[k], self.s1.at[k], self.r1.at[k], self.partner).wait_recv()
        self.send_next()
        if k:
            own = self.own(k)
            own[...] = (own[...].astype(F32) + self.land[k].astype(F32)).astype(BF16)
            copy = self.remote(
                own, self.got.at[k - 1], self.s2.at[k - 1], self.r2.at[k - 1], 2 * self.target(k) + self.minor
            )
            copy.start()
            self.copies.append(copy)

    def finish(self):
        total = self.own(0)[...].astype(F32) + self.land[0].astype(F32)
        for k in range(1, self.groups):
            slot = self.got.at[k - 1]
            self.remote(slot, slot, self.s2.at[k - 1], self.r2.at[k - 1], self.partner).wait_recv()
            total = total + self.got[k - 1].astype(F32)
        return total.astype(BF16)

    def drain(self):
        for copy in self.copies:
            copy.wait_send()


def layer_kernel(ranks, groups_dp, exp_dev, cap, *refs):
    (ids_in, tok_in, cot_in, wg_in, wu_in, wd_in), refs = refs[:6], refs[6:]
    (out_o, out_t, out_g, out_u, out_d), refs = refs[:5], refs[5:]
    (ids_all, x_all, c_all, wg, wu, wd, pick, pick_w, x_rows, do_rows, eo), refs = refs[:11], refs[11:]
    (pre_g, pre_u, hid, gg, ug, wpart, land_e, got_e, land_w, got_w), refs = refs[:10], refs[10:]
    (g_send, g_recv, g_local, w_sem), refs = refs[:4], refs[4:]
    sems_e, sems_w = refs[:4], refs[4:]
    rows = tok_in.shape[0]
    span = wpart.shape[-1]
    groups = ranks // 2
    chunk = min(8, ranks) * cap
    parts = [slice(i, i + chunk) for i in range(0, ranks * cap, chunk)]

    loads = [pltpu.make_async_copy(a, b, w_sem.at[i]) for i, (a, b) in enumerate(((wg_in, wg), (wu_in, wu), (wd_in, wd)))]
    for load in loads:
        load.start()
    greet([("expert", ranks), ("dp", groups_dp)])
    g_ids, g_tok, g_cot = [
        Gather(ranks, src, out, g_send.at[t], g_recv.at[t], g_local.at[t])
        for t, (src, out) in enumerate(((ids_in, ids_all), (tok_in, x_all), (cot_in, c_all)))
    ]
    g_ids.start()
    g_tok.start()
    for k in range(1, groups):
        g_ids.forward(k)
    g_ids.finish()

    first = lax.axis_index("expert") * exp_dev
    sub = lax.broadcasted_iota(jnp.int32, (8, rows), 0)
    earlier = (
        lax.broadcasted_iota(jnp.int32, (rows, rows), 0) < lax.broadcasted_iota(jnp.int32, (rows, rows), 1)
    ).astype(F32).astype(BF16)
    slots = lax.broadcasted_iota(jnp.int32, (cap, rows), 0).astype(F32)

    def place(b, carry):
        packed = ids_all[b]
        named, num = packed >> 9, packed & 511
        match = jnp.zeros((8, rows), F32)
        weight = jnp.zeros((8, rows), F32)
        for k in range(packed.shape[0]):
            hit = named[k : k + 1, :] == first + sub
            match = match + jnp.where(hit, 1.0, 0.0)
            weight = weight + jnp.where(hit, num[k : k + 1, :].astype(F32), 0.0)
        weight = weight / DENOM
        rank = dot(match.astype(BF16), earlier, 1, 0)
        slot = jnp.where(match > 0.0, rank, -1.0)
        for e in range(exp_dev):
            here = slot[e : e + 1, :] == slots
            pick[b, e * cap : (e + 1) * cap, :] = jnp.where(here, 1.0, 0.0).astype(BF16)
            pick_w[b, e * cap : (e + 1) * cap, :] = jnp.where(here, weight[e : e + 1, :], 0.0).astype(BF16)
        return carry

    lax.fori_loop(0, ranks, place, 0)

    def to_slots(sel, vals, into):
        def one(b, carry):
            got = dot(sel[b], vals[b], 1, 0).astype(BF16)
            for e in range(exp_dev):
                into[e, pl.ds(pl.multiple_of(b * cap, cap), cap), :] = got[e * cap : (e + 1) * cap, :]
            return carry

        lax.fori_loop(0, ranks, one, 0)

    def from_slots(sel, vals, into):
        def one(b, carry):
            here = jnp.concatenate(
                [vals[e, pl.ds(pl.multiple_of(b * cap, cap), cap), :] for e in range(exp_dev)], axis=0
            )
            into[b] = dot(sel[b], here, 0, 0).astype(BF16)
            return carry

        lax.fori_loop(0, ranks, one, 0)

    for k in range(1, groups):
        g_tok.forward(k)
    g_cot.start()
    g_tok.finish()
    to_slots(pick, x_all, x_rows)
    for load in loads:
        load.wait()
    ahead = list(range(1, groups))
    for e in range(exp_dev):
        for part in parts:
            xr = x_rows[e, part, :]
            gate = dot(xr, wg[e], 1, 0)
            up = dot(xr, wu[e], 1, 0)
            pre_g[e, part, :] = gate
            pre_u[e, part, :] = up
            hid[e, part, :] = (gate * jax.nn.sigmoid(gate) * up).astype(BF16)
        if ahead:
            g_cot.forward(ahead.pop(0))
        for part in parts:
            eo[e, part, :] = dot(hid[e, part, :], wd[e], 1, 0).astype(BF16)
    for k in ahead:
        g_cot.forward(k)
    g_tok.drain()
    from_slots(pick_w, eo, x_all)
    job_o, job_t = [
        Job("expert", ranks, part, land_e.at[j], got_e.at[j], [s.at[j] for s in sems_e], 2)
        for j, part in enumerate((x_all, c_all))
    ]
    job_o.exchange()
    g_cot.finish()
    to_slots(pick_w, c_all, do_rows)

    w_jobs = []
    for e in range(exp_dev):
        mine = [
            Job("dp", groups_dp, wpart.at[j, e], land_w.at[j, e], got_w.at[j, e], [s.at[j, e] for s in sems_w], groups_dp)
            for j in range(3)
        ]
        for part in parts:
            gate, up = pre_g[e, part, :], pre_u[e, part, :]
            hidden_grad = dot(do_rows[e, part, :], wd[e], 1, 1)
            sig = jax.nn.sigmoid(gate)
            gg[part, :] = (hidden_grad * up * sig * (1.0 + gate * (1.0 - sig))).astype(BF16)
            ug[part, :] = (hidden_grad * (gate * sig)).astype(BF16)
        for j, (left, right) in ((2, (hid[e], do_rows)), (0, (gg[...], x_rows)), (1, (ug[...], x_rows))):
            for i in range(groups_dp):
                wpart[j, e, i] = dot(left, right[e, :, i * span : (i + 1) * span], 0, 0).astype(BF16)
            mine[j].exchange()
        for part in parts:
            eo[e, part, :] = (dot(gg[part, :], wg[e], 1, 1) + dot(ug[part, :], wu[e], 1, 1)).astype(BF16)
        job_o.sum_next()
        for job in w_jobs[3 * e - 3 :]:
            for _ in range(job.groups):
                job.sum_next()
        w_jobs += mine
    g_cot.drain()
    from_slots(pick, eo, c_all)
    job_t.exchange()
    for job in w_jobs[-3:]:
        for _ in range(job.groups):
            job.sum_next()
    for _ in range(groups):
        job_o.sum_next()
    for _ in range(groups):
        job_t.sum_next()
    out_o[...] = job_o.finish()
    out_t[...] = job_t.finish()
    for n, job in enumerate(w_jobs):
        (out_g, out_u, out_d)[n % 3][n // 3] = job.finish()
    for job in [g_ids, job_o, job_t] + w_jobs:
        job.drain()


def local(tokens, expert_ids, route_num, w_gate, w_up, w_down, cotangent):
    ranks, groups_dp = lax.axis_size("expert"), lax.axis_size("dp")
    exp_dev, width, ff = w_gate.shape
    rows = tokens.shape[0]
    capacity = 5 * rows // 16
    cap = -(-capacity // 16) * 16
    span = width // groups_dp
    m_e, m_d = ranks // 2, groups_dp // 2
    packed = (expert_ids * 512 + route_num).T

    def sems(lead, groups):
        return [pltpu.SemaphoreType.DMA((*lead, groups)) for _ in range(4)]

    grad_t = jax.ShapeDtypeStruct((exp_dev, ff, span), BF16)
    out, tgrad, gate_t, up_t, down = pl.pallas_call(
        functools.partial(layer_kernel, ranks, groups_dp, exp_dev, cap),
        out_shape=[jax.ShapeDtypeStruct((rows, width), BF16)] * 2 + [grad_t] * 3,
        in_specs=[ANY] * 6,
        out_specs=[VMEM] * 5,
        scratch_shapes=[
            pltpu.VMEM((ranks, *packed.shape), jnp.int32),
            pltpu.VMEM((ranks, rows, width), BF16),
            pltpu.VMEM((ranks, rows, width), BF16),
            pltpu.VMEM(w_gate.shape, BF16),
            pltpu.VMEM(w_up.shape, BF16),
            pltpu.VMEM(w_down.shape, BF16),
            pltpu.VMEM((ranks, exp_dev * cap, rows), BF16),
            pltpu.VMEM((ranks, exp_dev * cap, rows), BF16),
            pltpu.VMEM((exp_dev, ranks * cap, width), BF16),
            pltpu.VMEM((exp_dev, ranks * cap, width), BF16),
            pltpu.VMEM((exp_dev, ranks * cap, width), BF16),
            pltpu.VMEM((exp_dev, ranks * cap, ff), F32),
            pltpu.VMEM((exp_dev, ranks * cap, ff), F32),
            pltpu.VMEM((exp_dev, ranks * cap, ff), BF16),
            pltpu.VMEM((ranks * cap, ff), BF16),
            pltpu.VMEM((ranks * cap, ff), BF16),
            pltpu.VMEM((3, exp_dev, groups_dp, ff, span), BF16),
            pltpu.VMEM((2, m_e, rows, width), BF16),
            pltpu.VMEM((2, m_e - 1, rows, width), BF16),
            pltpu.VMEM((3, exp_dev, m_d, ff, span), BF16),
            pltpu.VMEM((3, exp_dev, m_d - 1, ff, span), BF16),
            pltpu.SemaphoreType.DMA((3, ranks)),
            pltpu.SemaphoreType.DMA((3, ranks)),
            pltpu.SemaphoreType.DMA((3,)),
            pltpu.SemaphoreType.DMA((3,)),
            *sems((2,), m_e),
            *sems((3, exp_dev), m_d),
        ],
        compiler_params=pltpu.CompilerParams(
            collective_id=0, has_side_effects=True, vmem_limit_bytes=60 * 1024 * 1024
        ),
    )(packed, tokens, cotangent, w_gate, w_up, w_down)
    return out, tgrad, gate_t.transpose(0, 2, 1), up_t.transpose(0, 2, 1), down


def solution(mesh):
    in_specs = (
        P(("dp", "expert"), None),
        P(("dp", "expert"), None),
        P(("dp", "expert"), None),
        P("expert", None, None),
        P("expert", None, None),
        P("expert", None, None),
        P(("dp", "expert"), None),
    )
    out_specs = (
        P(("dp", "expert"), None),
        P(("dp", "expert"), None),
        P("expert", "dp", None),
        P("expert", "dp", None),
        P("expert", None, "dp"),
    )
    return jax.shard_map(local, mesh=mesh, in_specs=in_specs, out_specs=out_specs, check_vma=False)
```

```python
import functools

import jax
import jax.numpy as jnp
from jax import lax
from jax.experimental import pallas as pl
from jax.experimental.pallas import tpu as pltpu
from jax.sharding import PartitionSpec as P

DENOM = 256
MESH = pl.DeviceIdType.MESH
ANY = pl.BlockSpec(memory_space=pl.ANY)
VMEM = pl.BlockSpec(memory_space=pltpu.VMEM)
BF16, F32 = jnp.bfloat16, jnp.float32


def split_index(axis, size):
    me = lax.axis_index(axis)
    return me // 2, lax.rem(me, 2), size // 2


def greet(axes):
    barrier = pltpu.get_barrier_semaphore()
    count = 0
    for axis, size in axes:
        major, minor, groups = split_index(axis, size)
        peers = [2 * major + 1 - minor]
        peers += [2 * lax.rem(major + k, groups) + minor for k in range(1, groups)]
        for peer in peers:
            pl.semaphore_signal(barrier, inc=1, device_id={axis: peer}, device_id_type=MESH)
        count += len(peers)
    pl.semaphore_wait(barrier, count)


def near_first(groups):
    return sorted(range(1, groups), key=lambda k: min(k, groups - k))


def dot(a, b, ca, cb):
    return lax.dot_general(a, b, (((ca,), (cb,)), ((), ())), preferred_element_type=F32)


class Gather:
    def __init__(self, ranks, src, out, part, send, recv, local_sem):
        self.src, self.out, self.part, self.send, self.recv = src.at[part], out, part, send, recv
        self.major, self.minor, self.groups = split_index("expert", ranks)
        self.me = 2 * self.major + self.minor
        self.partner = 2 * self.major + 1 - self.minor
        self.copies = []
        self.keep = pltpu.make_async_copy(self.src, self.at(self.me), local_sem)

    def at(self, shard):
        return self.out.at[shard, self.part]

    def push(self, src, shard, slot, peer):
        copy = pltpu.make_async_remote_copy(
            src_ref=src, dst_ref=self.at(shard), send_sem=self.send.at[slot], recv_sem=self.recv.at[shard],
            device_id={"expert": peer}, device_id_type=MESH,
        )
        copy.start()
        return copy

    def arrived(self, shard):
        pltpu.make_async_remote_copy(
            src_ref=self.at(shard), dst_ref=self.at(shard), send_sem=self.send.at[0],
            recv_sem=self.recv.at[shard], device_id={"expert": self.partner}, device_id_type=MESH,
        ).wait_recv()

    def to_peer(self, k):
        self.peer_copy = self.push(self.src, self.me, k, 2 * lax.rem(self.major + k, self.groups) + self.minor)

    def start(self):
        self.to_peer(near_first(self.groups)[0])
        self.copies.append(self.push(self.src, self.me, 0, self.partner))
        self.keep.start()

    def sent(self):
        for copy in self.copies:
            copy.wait_send()
        self.copies = []

    def forward(self, k):
        shard = 2 * lax.rem(self.major - k + self.groups, self.groups) + self.minor
        self.arrived(shard)
        self.copies.append(self.push(self.at(shard), shard, self.groups + k - 1, self.partner))

    def finish(self):
        for k in range(self.groups):
            self.arrived(2 * lax.rem(self.major - k + self.groups, self.groups) + 1 - self.minor)
        self.keep.wait()


def gather_step(halves, i, following=()):
    order = near_first(halves[0].groups)
    last = i + 1 == len(order)
    for g in halves:
        g.peer_copy.wait_send()
        if not last:
            g.to_peer(order[i + 1])
    for g in following if last else ():
        g.start()
    for g in halves:
        g.forward(order[i])


class Job:
    def __init__(self, axis, size, source, land, got, sems, window, part=slice(None)):
        self.part = part
        self.axis, self.source, self.land, self.got, self.window = axis, source, land, got, window
        self.s1, self.r1, self.s2, self.r2 = sems
        self.major, self.minor, self.groups = split_index(axis, size)
        self.partner = 2 * self.major + 1 - self.minor
        self.copies = []
        self.unsent = near_first(self.groups)[::-1] + [0]
        self.unsummed = list(self.unsent)

    def remote(self, src, dst, s, r, peer):
        return pltpu.make_async_remote_copy(
            src_ref=src, dst_ref=dst, send_sem=s, recv_sem=r, device_id={self.axis: peer}, device_id_type=MESH
        )

    def target(self, k):
        return lax.rem(self.major + k, self.groups)

    def own(self, k):
        return self.source.at[2 * self.target(k) + self.minor, self.part]

    def send_next(self):
        if self.unsent:
            k = self.unsent.pop(0)
            copy = self.remote(
                self.source.at[2 * self.target(k) + 1 - self.minor, self.part], self.land.at[k], self.s1.at[k], self.r1.at[k],
                self.partner,
            )
            copy.start()
            self.copies.append(copy)

    def exchange(self):
        for _ in range(self.window):
            self.send_next()

    def sum_next(self):
        if not self.unsummed:
            return
        k = self.unsummed.pop(0)
        self.remote(self.land.at[k], self.land.at[k], self.s1.at[k], self.r1.at[k], self.partner).wait_recv()
        self.send_next()
        if k:
            own = self.own(k)
            own[...] = (own[...].astype(F32) + self.land[k].astype(F32)).astype(BF16)
            copy = self.remote(
                own, self.got.at[k - 1], self.s2.at[k - 1], self.r2.at[k - 1], 2 * self.target(k) + self.minor
            )
            copy.start()
            self.copies.append(copy)

    def sum_ahead(self):
        for _ in range(self.groups - 1):
            self.sum_next()

    def finish(self):
        total = self.own(0)[...].astype(F32) + self.land[0].astype(F32)
        for k in range(1, self.groups):
            slot = self.got.at[k - 1]
            self.remote(slot, slot, self.s2.at[k - 1], self.r2.at[k - 1], self.partner).wait_recv()
            total = total + self.got[k - 1].astype(F32)
        return total

    def drain(self):
        for copy in self.copies:
            copy.wait_send()


def layer_kernel(ranks, groups_dp, exp_dev, cap, *refs):
    (ids_in, tok_in, cot_in, wg_in, wu_in, wd_in), refs = refs[:6], refs[6:]
    (out_o, out_t, out_g, out_u, out_d), refs = refs[:5], refs[5:]
    (ids_all, x_all, c_all, wg, wu, wd, pick, pick_w, x_rows, do_rows, eo), refs = refs[:11], refs[11:]
    (pre_g, pre_u, hid, gg, ug, wpart, land_e, got_e, land_w, got_w), refs = refs[:10], refs[10:]
    (g_send, g_recv, g_local, w_sem), refs = refs[:4], refs[4:]
    sems_e, sems_w = refs[:4], refs[4:]
    rows = tok_in.shape[0]
    span = wpart.shape[-1]
    groups = ranks // 2
    chunk = min(8, ranks) * cap
    parts = [slice(i, i + chunk) for i in range(0, ranks * cap, chunk)]

    loads = [pltpu.make_async_copy(a, b, w_sem.at[i]) for i, (a, b) in enumerate(((wg_in, wg), (wu_in, wu), (wd_in, wd)))]
    for load in loads:
        load.start()
    greet([("expert", ranks), ("dp", groups_dp)])
    half = rows // 2
    halves = (slice(0, half), slice(half, rows))

    def gather(t, src, out, part):
        return Gather(ranks, src, out, part, g_send.at[t], g_recv.at[t], g_local.at[t])

    g_ids = [gather(0, ids_in, ids_all, slice(None))]
    g_tok = [gather(1 + h, tok_in, x_all, halves[h]) for h in range(2)]
    g_cot = [gather(3 + h, cot_in, c_all, halves[h]) for h in range(2)]
    steps = range(groups - 1)
    for g in g_ids + g_tok:
        g.start()
    for i in steps:
        gather_step(g_ids, i)
    g_ids[0].finish()

    first = lax.axis_index("expert") * exp_dev
    sub = lax.broadcasted_iota(jnp.int32, (8, rows), 0)
    earlier = (
        lax.broadcasted_iota(jnp.int32, (rows, rows), 0) < lax.broadcasted_iota(jnp.int32, (rows, rows), 1)
    ).astype(F32).astype(BF16)
    slots = lax.broadcasted_iota(jnp.int32, (cap, rows), 0).astype(F32)

    def place(b, carry):
        packed = ids_all[b]
        named, num = packed >> 9, packed & 511
        match = jnp.zeros((8, rows), F32)
        weight = jnp.zeros((8, rows), F32)
        for k in range(packed.shape[0]):
            hit = named[k : k + 1, :] == first + sub
            match = match + jnp.where(hit, 1.0, 0.0)
            weight = weight + jnp.where(hit, num[k : k + 1, :].astype(F32), 0.0)
        weight = weight / DENOM
        rank = dot(match.astype(BF16), earlier, 1, 0)
        slot = jnp.where(match > 0.0, rank, -1.0)
        for e in range(exp_dev):
            here = slot[e : e + 1, :] == slots
            pick[b, e * cap : (e + 1) * cap, :] = jnp.where(here, 1.0, 0.0).astype(BF16)
            pick_w[b, e * cap : (e + 1) * cap, :] = jnp.where(here, weight[e : e + 1, :], 0.0).astype(BF16)
        return carry

    lax.fori_loop(0, ranks, place, 0)

    def to_slots(sel, vals, into):
        def one(b, carry):
            got = dot(sel[b], vals[b], 1, 0).astype(BF16)
            for e in range(exp_dev):
                into[e, pl.ds(pl.multiple_of(b * cap, cap), cap), :] = got[e * cap : (e + 1) * cap, :]
            return carry

        lax.fori_loop(0, ranks, one, 0)

    def from_slots(sel, vals, into):
        def one(b, carry):
            here = jnp.concatenate(
                [vals[e, pl.ds(pl.multiple_of(b * cap, cap), cap), :] for e in range(exp_dev)], axis=0
            )
            into[b] = dot(sel[b], here, 0, 0).astype(BF16)
            return carry

        lax.fori_loop(0, ranks, one, 0)

    for i in steps:
        gather_step(g_tok, i, g_cot)
    for g in g_tok:
        g.finish()
    to_slots(pick, x_all, x_rows)
    for load in loads:
        load.wait()
    ahead = list(steps)
    for e in range(exp_dev):
        for part in parts:
            xr = x_rows[e, part, :]
            gate = dot(xr, wg[e], 1, 0)
            up = dot(xr, wu[e], 1, 0)
            pre_g[e, part, :] = gate
            pre_u[e, part, :] = up
            hid[e, part, :] = (gate * jax.nn.sigmoid(gate) * up).astype(BF16)
        if ahead:
            gather_step(g_cot, ahead.pop(0))
        for part in parts:
            eo[e, part, :] = dot(hid[e, part, :], wd[e], 1, 0).astype(BF16)
    for i in ahead:
        gather_step(g_cot, i)
    for g in g_tok:
        g.sent()
    from_slots(pick_w, eo, x_all)
    jobs_o, jobs_t = [
        [
            Job("expert", ranks, whole, land_e.at[j, h], got_e.at[j, h], [s.at[j, h] for s in sems_e], 1, halves[h])
            for h in range(2)
        ]
        for j, whole in enumerate((x_all, c_all))
    ]
    for job in jobs_o:
        job.exchange()
    for g in g_cot:
        g.finish()
    to_slots(pick_w, c_all, do_rows)

    w_jobs = []
    for e in range(exp_dev):
        mine = [
            Job("dp", groups_dp, wpart.at[j, e], land_w.at[j, e], got_w.at[j, e], [s.at[j, e] for s in sems_w], groups_dp)
            for j in range(3)
        ]
        def weight_part(j, left, right):
            for i in range(groups_dp):
                wpart[j, e, i] = dot(left, right[e, :, i * span : (i + 1) * span], 0, 0).astype(BF16)
            mine[j].exchange()

        weight_part(2, hid[e], do_rows)
        for part in parts:
            gate, up = pre_g[e, part, :], pre_u[e, part, :]
            hidden_grad = dot(do_rows[e, part, :], wd[e], 1, 1)
            sig = jax.nn.sigmoid(gate)
            gg[part, :] = (hidden_grad * up * sig * (1.0 + gate * (1.0 - sig))).astype(BF16)
            ug[part, :] = (hidden_grad * (gate * sig)).astype(BF16)
        mine[2].sum_ahead()
        weight_part(0, gg[...], x_rows)
        weight_part(1, ug[...], x_rows)
        mine[0].sum_ahead()
        for part in parts:
            eo[e, part, :] = (dot(gg[part, :], wg[e], 1, 1) + dot(ug[part, :], wu[e], 1, 1)).astype(BF16)
        mine[1].sum_ahead()
        for job in jobs_o:
            job.sum_next()
        w_jobs += mine
    for g in g_cot:
        g.sent()
    from_slots(pick, eo, c_all)
    for job in jobs_t:
        job.exchange()
    for jobs in (jobs_o, jobs_t):
        for _ in range(groups):
            for job in jobs:
                job.sum_next()
    for job in w_jobs:
        job.sum_next()
    for n, job in enumerate(w_jobs):
        total = job.finish()
        if n % 3 == 2:
            out_d[n // 3] = total.astype(BF16)
        else:
            (out_g, out_u)[n % 3][n // 3] = total.T.astype(BF16)
    for jobs, out in ((jobs_o, out_o), (jobs_t, out_t)):
        for job in jobs:
            out[job.part, :] = job.finish().astype(BF16)
    for job in jobs_o + jobs_t + w_jobs:
        job.drain()
    for g in g_ids:
        g.sent()


def copy_kernel(*refs):
    copies = [pltpu.make_async_copy(a, b, refs[10].at[i]) for i, (a, b) in enumerate(zip(refs[:5], refs[5:10]))]
    for copy in copies:
        copy.start()
    for copy in copies:
        copy.wait()


def local(tokens, expert_ids, route_num, w_gate, w_up, w_down, cotangent):
    ranks, groups_dp = lax.axis_size("expert"), lax.axis_size("dp")
    exp_dev, width, ff = w_gate.shape
    rows = tokens.shape[0]
    capacity = 5 * rows // 16
    cap = -(-capacity // 16) * 16
    span = width // groups_dp
    m_e, m_d = ranks // 2, groups_dp // 2
    packed = (expert_ids * 512 + route_num).T

    def sems(lead, groups):
        return [pltpu.SemaphoreType.DMA((*lead, groups)) for _ in range(4)]

    grad = jax.ShapeDtypeStruct((exp_dev, span, ff), BF16)
    out_shape = [jax.ShapeDtypeStruct((rows, width), BF16)] * 2 + [grad] * 2
    out_shape += [jax.ShapeDtypeStruct((exp_dev, ff, span), BF16)]
    results = pl.pallas_call(
        functools.partial(layer_kernel, ranks, groups_dp, exp_dev, cap),
        out_shape=out_shape,
        in_specs=[ANY] * 6,
        out_specs=[VMEM] * 5,
        scratch_shapes=[
            pltpu.VMEM((ranks, *packed.shape), jnp.int32),
            pltpu.VMEM((ranks, rows, width), BF16),
            pltpu.VMEM((ranks, rows, width), BF16),
            pltpu.VMEM(w_gate.shape, BF16),
            pltpu.VMEM(w_up.shape, BF16),
            pltpu.VMEM(w_down.shape, BF16),
            pltpu.VMEM((ranks, exp_dev * cap, rows), BF16),
            pltpu.VMEM((ranks, exp_dev * cap, rows), BF16),
            pltpu.VMEM((exp_dev, ranks * cap, width), BF16),
            pltpu.VMEM((exp_dev, ranks * cap, width), BF16),
            pltpu.VMEM((exp_dev, ranks * cap, width), BF16),
            pltpu.VMEM((exp_dev, ranks * cap, ff), F32),
            pltpu.VMEM((exp_dev, ranks * cap, ff), F32),
            pltpu.VMEM((exp_dev, ranks * cap, ff), BF16),
            pltpu.VMEM((ranks * cap, ff), BF16),
            pltpu.VMEM((ranks * cap, ff), BF16),
            pltpu.VMEM((3, exp_dev, groups_dp, ff, span), BF16),
            pltpu.VMEM((2, 2, m_e, rows // 2, width), BF16),
            pltpu.VMEM((2, 2, m_e - 1, rows // 2, width), BF16),
            pltpu.VMEM((3, exp_dev, m_d, ff, span), BF16),
            pltpu.VMEM((3, exp_dev, m_d - 1, ff, span), BF16),
            pltpu.SemaphoreType.DMA((5, ranks)),
            pltpu.SemaphoreType.DMA((5, ranks)),
            pltpu.SemaphoreType.DMA((5,)),
            pltpu.SemaphoreType.DMA((3,)),
            *sems((2, 2), m_e),
            *sems((3, exp_dev), m_d),
        ],
        compiler_params=pltpu.CompilerParams(
            collective_id=0, has_side_effects=True, vmem_limit_bytes=60 * 1024 * 1024
        ),
    )(packed, tokens, cotangent, w_gate, w_up, w_down)
    return tuple(pl.pallas_call(
        copy_kernel, out_shape=out_shape, in_specs=[ANY] * 5, out_specs=[ANY] * 5,
        scratch_shapes=[pltpu.SemaphoreType.DMA((5,))],
    )(*results))


def solution(mesh):
    in_specs = (
        P(("dp", "expert"), None),
        P(("dp", "expert"), None),
        P(("dp", "expert"), None),
        P("expert", None, None),
        P("expert", None, None),
        P("expert", None, None),
        P(("dp", "expert"), None),
    )
    out_specs = (
        P(("dp", "expert"), None),
        P(("dp", "expert"), None),
        P("expert", "dp", None),
        P("expert", "dp", None),
        P("expert", None, "dp"),
    )
    return jax.shard_map(local, mesh=mesh, in_specs=in_specs, out_specs=out_specs, check_vma=False)
```

```python
import functools

import jax
import jax.numpy as jnp
from jax import lax
from jax.experimental import pallas as pl
from jax.experimental.pallas import tpu as pltpu
from jax.sharding import PartitionSpec as P

DENOM = 256
MESH = pl.DeviceIdType.MESH
ANY = pl.BlockSpec(memory_space=pl.ANY)
VMEM = pl.BlockSpec(memory_space=pltpu.VMEM)
BF16, F32 = jnp.bfloat16, jnp.float32


def split_index(axis, size):
    me = lax.axis_index(axis)
    return me // 2, lax.rem(me, 2), size // 2


def greet(axes):
    barrier = pltpu.get_barrier_semaphore()
    count = 0
    for axis, size in axes:
        major, minor, groups = split_index(axis, size)
        peers = [2 * major + 1 - minor]
        peers += [2 * lax.rem(major + k, groups) + minor for k in range(1, groups)]
        for peer in peers:
            pl.semaphore_signal(barrier, inc=1, device_id={axis: peer}, device_id_type=MESH)
        count += len(peers)
    pl.semaphore_wait(barrier, count)


def near_first(groups):
    return sorted(range(1, groups), key=lambda k: min(k, groups - k))


def dot(a, b, ca, cb):
    return lax.dot_general(a, b, (((ca,), (cb,)), ((), ())), preferred_element_type=F32)


class Gather:
    def __init__(self, ranks, src, out, part, send, recv, local_sem):
        self.src, self.out, self.part, self.send, self.recv = src.at[part], out, part, send, recv
        self.major, self.minor, self.groups = split_index("expert", ranks)
        self.me = 2 * self.major + self.minor
        self.partner = 2 * self.major + 1 - self.minor
        self.copies = []
        self.keep = pltpu.make_async_copy(self.src, self.at(self.me), local_sem)

    def at(self, shard):
        return self.out.at[(shard, *self.part)]

    def push(self, src, shard, slot, peer):
        copy = pltpu.make_async_remote_copy(
            src_ref=src, dst_ref=self.at(shard), send_sem=self.send.at[slot], recv_sem=self.recv.at[shard],
            device_id={"expert": peer}, device_id_type=MESH,
        )
        copy.start()
        return copy

    def arrived(self, shard):
        pltpu.make_async_remote_copy(
            src_ref=self.at(shard), dst_ref=self.at(shard), send_sem=self.send.at[0],
            recv_sem=self.recv.at[shard], device_id={"expert": self.partner}, device_id_type=MESH,
        ).wait_recv()

    def start(self):
        self.keep.start()
        self.copies.append(self.push(self.src, self.me, 0, self.partner))
        for k in near_first(self.groups):
            peer = 2 * lax.rem(self.major + k, self.groups) + self.minor
            self.copies.append(self.push(self.src, self.me, k, peer))

    def sent(self):
        for copy in self.copies:
            copy.wait_send()
        self.copies = []

    def forward(self, k):
        shard = 2 * lax.rem(self.major - k + self.groups, self.groups) + self.minor
        self.arrived(shard)
        self.copies.append(self.push(self.at(shard), shard, self.groups + k - 1, self.partner))

    def finish(self):
        for k in range(self.groups):
            self.arrived(2 * lax.rem(self.major - k + self.groups, self.groups) + 1 - self.minor)
        self.keep.wait()


class Job:
    def __init__(self, axis, size, source, land, got, sems, window, part=slice(None)):
        self.part = part
        self.axis, self.source, self.land, self.got, self.window = axis, source, land, got, window
        self.s1, self.r1, self.s2, self.r2 = sems
        self.major, self.minor, self.groups = split_index(axis, size)
        self.partner = 2 * self.major + 1 - self.minor
        self.copies = []
        self.unsent = near_first(self.groups)[::-1] + [0]
        self.unsummed = list(self.unsent)

    def remote(self, src, dst, s, r, peer):
        return pltpu.make_async_remote_copy(
            src_ref=src, dst_ref=dst, send_sem=s, recv_sem=r, device_id={self.axis: peer}, device_id_type=MESH
        )

    def target(self, k):
        return lax.rem(self.major + k, self.groups)

    def own(self, k):
        return self.source.at[2 * self.target(k) + self.minor, self.part]

    def send_next(self):
        if self.unsent:
            k = self.unsent.pop(0)
            copy = self.remote(
                self.source.at[2 * self.target(k) + 1 - self.minor, self.part], self.land.at[k], self.s1.at[k], self.r1.at[k],
                self.partner,
            )
            copy.start()
            self.copies.append(copy)

    def exchange(self):
        for _ in range(self.window):
            self.send_next()

    def sum_next(self):
        if not self.unsummed:
            return
        k = self.unsummed.pop(0)
        self.remote(self.land.at[k], self.land.at[k], self.s1.at[k], self.r1.at[k], self.partner).wait_recv()
        if self.axis == "expert":
            self.send_next()
        if k:
            own = self.own(k)
            own[...] = (own[...].astype(F32) + self.land[k].astype(F32)).astype(BF16)
            copy = self.remote(
                own, self.got.at[k - 1], self.s2.at[k - 1], self.r2.at[k - 1], 2 * self.target(k) + self.minor
            )
            copy.start()
            self.copies.append(copy)

    def sum_ahead(self):
        for _ in range(self.groups - 1):
            self.sum_next()

    def finish(self):
        total = self.own(0)[...].astype(F32) + self.land[0].astype(F32)
        for k in range(1, self.groups):
            slot = self.got.at[k - 1]
            self.remote(slot, slot, self.s2.at[k - 1], self.r2.at[k - 1], self.partner).wait_recv()
            total = total + self.got[k - 1].astype(F32)
        return total

    def drain(self):
        for copy in self.copies:
            copy.wait_send()


def layer_kernel(ranks, groups_dp, exp_dev, cap, *refs):
    (ids_in, tok_in, cot_in, wg_in, wu_in, wd_in), refs = refs[:6], refs[6:]
    (out_o, out_t, out_g, out_u, out_d), refs = refs[:5], refs[5:]
    (ids_all, x_all, c_all, wg, wu, wd, pick, pick_w, x_rows, do_rows, eo), refs = refs[:11], refs[11:]
    (pre_g, pre_u, hid, gg, ug, wpart, land_e, got_e, land_w, got_w), refs = refs[:10], refs[10:]
    (g_send, g_recv, g_local, w_sem), refs = refs[:4], refs[4:]
    sems_e, sems_w = refs[:4], refs[4:]
    rows = tok_in.shape[0]
    span = wpart.shape[-1]
    groups = ranks // 2
    chunk = min(8, ranks) * cap
    parts = [slice(i, i + chunk) for i in range(0, ranks * cap, chunk)]

    loads = [pltpu.make_async_copy(a, b, w_sem.at[i]) for i, (a, b) in enumerate(((wg_in, wg), (wu_in, wu), (wd_in, wd)))]
    for load in loads:
        load.start()
    greet([("expert", ranks), ("dp", groups_dp)])
    half = rows // 2
    halves = (slice(0, half), slice(half, rows))

    def gather(t, src, out, part):
        return Gather(ranks, src, out, part, g_send.at[t], g_recv.at[t], g_local.at[t])

    dp_major, _, dp_groups = split_index("dp", groups_dp)
    wide = tok_in.shape[1] // 2
    later = dp_major // (dp_groups // 2)
    col_halves = [pl.ds(pl.multiple_of(c * wide, wide), wide) for c in (1 - later, later)]
    every = slice(None)
    g_ids = gather(0, ids_in, ids_all, (every, every))
    g_tok = [gather(1 + h, tok_in, x_all, (halves[h], every)) for h in range(2)]
    g_cot = [gather(3 + h, cot_in, c_all, (every, col_halves[h])) for h in range(2)]
    order = near_first(groups)
    for g in [g_ids] + g_tok:
        g.start()
    for k in order:
        g_ids.forward(k)
    g_ids.finish()

    first = lax.axis_index("expert") * exp_dev
    sub = lax.broadcasted_iota(jnp.int32, (8, rows), 0)
    earlier = (
        lax.broadcasted_iota(jnp.int32, (rows, rows), 0) < lax.broadcasted_iota(jnp.int32, (rows, rows), 1)
    ).astype(F32).astype(BF16)
    slots = lax.broadcasted_iota(jnp.int32, (cap, rows), 0).astype(F32)

    def place(b, carry):
        packed = ids_all[b]
        named, num = packed >> 9, packed & 511
        match = jnp.zeros((8, rows), F32)
        weight = jnp.zeros((8, rows), F32)
        for k in range(packed.shape[0]):
            hit = named[k : k + 1, :] == first + sub
            match = match + jnp.where(hit, 1.0, 0.0)
            weight = weight + jnp.where(hit, num[k : k + 1, :].astype(F32), 0.0)
        weight = weight / DENOM
        rank = dot(match.astype(BF16), earlier, 1, 0)
        slot = jnp.where(match > 0.0, rank, -1.0)
        for e in range(exp_dev):
            here = slot[e : e + 1, :] == slots
            pick[b, e * cap : (e + 1) * cap, :] = jnp.where(here, 1.0, 0.0).astype(BF16)
            pick_w[b, e * cap : (e + 1) * cap, :] = jnp.where(here, weight[e : e + 1, :], 0.0).astype(BF16)
        return carry

    lax.fori_loop(0, ranks, place, 0)

    def to_slots(sel, vals, into, cols):
        def one(b, carry):
            got = dot(sel[b], vals[b, :, cols], 1, 0).astype(BF16)
            for e in range(exp_dev):
                into[e, pl.ds(pl.multiple_of(b * cap, cap), cap), cols] = got[e * cap : (e + 1) * cap, :]
            return carry

        lax.fori_loop(0, ranks, one, 0)

    def from_slots(sel, vals, into):
        def one(b, carry):
            here = jnp.concatenate(
                [vals[e, pl.ds(pl.multiple_of(b * cap, cap), cap), :] for e in range(exp_dev)], axis=0
            )
            into[b] = dot(sel[b], here, 0, 0).astype(BF16)
            return carry

        lax.fori_loop(0, ranks, one, 0)

    for g, following in zip(g_tok, g_cot):
        for k in order:
            g.forward(k)
        following.start()
    for g in g_tok:
        g.finish()
    to_slots(pick, x_all, x_rows, every)
    for load in loads:
        load.wait()
    ahead = [(g, k) for g in g_cot for k in order]

    def forward_next():
        if ahead:
            g, k = ahead.pop(0)
            g.forward(k)

    for e in range(exp_dev):
        for part in parts:
            xr = x_rows[e, part, :]
            gate = dot(xr, wg[e], 1, 0)
            up = dot(xr, wu[e], 1, 0)
            pre_g[e, part, :] = gate
            pre_u[e, part, :] = up
            hid[e, part, :] = (gate * jax.nn.sigmoid(gate) * up).astype(BF16)
        forward_next()
        for part in parts:
            eo[e, part, :] = dot(hid[e, part, :], wd[e], 1, 0).astype(BF16)
        forward_next()
    while ahead:
        forward_next()
    for g in g_tok:
        g.sent()
    jobs_o, jobs_t = [
        [
            Job("expert", ranks, whole, land_e.at[j, h], got_e.at[j, h], [s.at[j, h] for s in sems_e], 1, halves[h])
            for h in range(2)
        ]
        for j, whole in enumerate((x_all, c_all))
    ]
    w_jobs = [
        Job("dp", groups_dp, wpart.at[j, e], land_w.at[j, e], got_w.at[j, e], [s.at[j, e] for s in sems_w], window)
        for e in range(exp_dev)
        for j, window in ((0, groups_dp), (1, groups_dp), (2, dp_groups - 1))
    ]

    def weight_block(j, e, left, right, i):
        cols = pl.ds(pl.multiple_of(i * span, span), span)
        wpart[j, e, i] = dot(left, right[e, :, cols], 0, 0).astype(BF16)

    def down_half(h):
        g_cot[h].finish()
        to_slots(pick_w, c_all, do_rows, col_halves[h])
        for e in range(exp_dev):
            for n in range(dp_groups):
                weight_block(2, e, hid[e], do_rows, (later if h else 1 - later) * dp_groups + n)
            if h == 0 and dp_groups == 2:
                w_jobs[3 * e + 2].exchange()

    down_half(0)
    from_slots(pick_w, eo, x_all)
    for job in jobs_o:
        job.exchange()
    if dp_groups == 2:
        for e in range(exp_dev):
            w_jobs[3 * e + 2].sum_ahead()
    down_half(1)
    for e in range(exp_dev):
        if dp_groups != 2:
            w_jobs[3 * e + 2].exchange()
        w_jobs[3 * e + 2].send_next()
    for e in range(exp_dev):
        mine = w_jobs[3 * e : 3 * e + 3]

        def weight_part(j, left, right):
            for i in range(groups_dp):
                weight_block(j, e, left, right, i)
            mine[j].exchange()

        for part in parts:
            gate, up = pre_g[e, part, :], pre_u[e, part, :]
            hidden_grad = dot(do_rows[e, part, :], wd[e], 1, 1)
            sig = jax.nn.sigmoid(gate)
            gg[part, :] = (hidden_grad * up * sig * (1.0 + gate * (1.0 - sig))).astype(BF16)
            ug[part, :] = (hidden_grad * (gate * sig)).astype(BF16)
        if dp_groups != 2:
            mine[2].sum_ahead()
        weight_part(0, gg[...], x_rows)
        weight_part(1, ug[...], x_rows)
        mine[0].sum_ahead()
        for part in parts:
            eo[e, part, :] = (dot(gg[part, :], wg[e], 1, 1) + dot(ug[part, :], wu[e], 1, 1)).astype(BF16)
        mine[1].sum_ahead()
        for job in jobs_o:
            job.sum_next()
    for g in g_cot:
        g.sent()
    from_slots(pick, eo, c_all)
    for job in jobs_t:
        job.exchange()
    for jobs in (jobs_o, jobs_t):
        for _ in range(groups):
            for job in jobs:
                job.sum_next()
    for job in w_jobs:
        job.sum_next()
    for n, job in enumerate(w_jobs):
        total = job.finish()
        if n % 3 == 2:
            out_d[n // 3] = total.astype(BF16)
        else:
            (out_g, out_u)[n % 3][n // 3] = total.T.astype(BF16)
    for jobs, out in ((jobs_o, out_o), (jobs_t, out_t)):
        for job in jobs:
            out[job.part, :] = job.finish().astype(BF16)
    for job in jobs_o + jobs_t + w_jobs:
        job.drain()
    g_ids.sent()


def copy_kernel(*refs):
    for a, b in zip(refs[:5], refs[5:]):
        b[...] = a[...]


def local(tokens, expert_ids, route_num, w_gate, w_up, w_down, cotangent):
    ranks, groups_dp = lax.axis_size("expert"), lax.axis_size("dp")
    exp_dev, width, ff = w_gate.shape
    rows = tokens.shape[0]
    capacity = 5 * rows // 16
    cap = -(-capacity // 16) * 16
    span = width // groups_dp
    m_e, m_d = ranks // 2, groups_dp // 2
    packed = (expert_ids * 512 + route_num).T

    def sems(lead, groups):
        return [pltpu.SemaphoreType.DMA((*lead, groups)) for _ in range(4)]

    grad = jax.ShapeDtypeStruct((exp_dev, span, ff), BF16)
    out_shape = [jax.ShapeDtypeStruct((rows, width), BF16)] * 2 + [grad] * 2
    out_shape += [jax.ShapeDtypeStruct((exp_dev, ff, span), BF16)]
    results = pl.pallas_call(
        functools.partial(layer_kernel, ranks, groups_dp, exp_dev, cap),
        out_shape=out_shape,
        in_specs=[ANY] * 6,
        out_specs=[VMEM] * 5,
        scratch_shapes=[
            pltpu.VMEM((ranks, *packed.shape), jnp.int32),
            pltpu.VMEM((ranks, rows, width), BF16),
            pltpu.VMEM((ranks, rows, width), BF16),
            pltpu.VMEM(w_gate.shape, BF16),
            pltpu.VMEM(w_up.shape, BF16),
            pltpu.VMEM(w_down.shape, BF16),
            pltpu.VMEM((ranks, exp_dev * cap, rows), BF16),
            pltpu.VMEM((ranks, exp_dev * cap, rows), BF16),
            pltpu.VMEM((exp_dev, ranks * cap, width), BF16),
            pltpu.VMEM((exp_dev, ranks * cap, width), BF16),
            pltpu.VMEM((exp_dev, ranks * cap, width), BF16),
            pltpu.VMEM((exp_dev, ranks * cap, ff), F32),
            pltpu.VMEM((exp_dev, ranks * cap, ff), F32),
            pltpu.VMEM((exp_dev, ranks * cap, ff), BF16),
            pltpu.VMEM((ranks * cap, ff), BF16),
            pltpu.VMEM((ranks * cap, ff), BF16),
            pltpu.VMEM((3, exp_dev, groups_dp, ff, span), BF16),
            pltpu.VMEM((2, 2, m_e, rows // 2, width), BF16),
            pltpu.VMEM((2, 2, m_e - 1, rows // 2, width), BF16),
            pltpu.VMEM((3, exp_dev, m_d, ff, span), BF16),
            pltpu.VMEM((3, exp_dev, m_d - 1, ff, span), BF16),
            pltpu.SemaphoreType.DMA((5, ranks)),
            pltpu.SemaphoreType.DMA((5, ranks)),
            pltpu.SemaphoreType.DMA((5,)),
            pltpu.SemaphoreType.DMA((3,)),
            *sems((2, 2), m_e),
            *sems((3, exp_dev), m_d),
        ],
        compiler_params=pltpu.CompilerParams(
            collective_id=0, has_side_effects=True, vmem_limit_bytes=60 * 1024 * 1024
        ),
    )(packed, tokens, cotangent, w_gate, w_up, w_down)
    return tuple(pl.pallas_call(
        copy_kernel, out_shape=out_shape, in_specs=[VMEM] * 5, out_specs=[VMEM] * 5,
        compiler_params=pltpu.CompilerParams(vmem_limit_bytes=16 * 1024 * 1024),
    )(*results))


def solution(mesh):
    in_specs = (
        P(("dp", "expert"), None),
        P(("dp", "expert"), None),
        P(("dp", "expert"), None),
        P("expert", None, None),
        P("expert", None, None),
        P("expert", None, None),
        P(("dp", "expert"), None),
    )
    out_specs = (
        P(("dp", "expert"), None),
        P(("dp", "expert"), None),
        P("expert", "dp", None),
        P("expert", "dp", None),
        P("expert", None, "dp"),
    )
    return jax.shard_map(local, mesh=mesh, in_specs=in_specs, out_specs=out_specs, check_vma=False)
```

```python
import functools

import jax
import jax.numpy as jnp
from jax import lax
from jax.experimental import pallas as pl
from jax.experimental.pallas import tpu as pltpu
from jax.sharding import PartitionSpec as P

DENOM = 256
MESH = pl.DeviceIdType.MESH
ANY = pl.BlockSpec(memory_space=pl.ANY)
VMEM = pl.BlockSpec(memory_space=pltpu.VMEM)
BF16, F32 = jnp.bfloat16, jnp.float32


def split_index(axis, size):
    me = lax.axis_index(axis)
    return me // 2, lax.rem(me, 2), size // 2


def greet(axes):
    barrier = pltpu.get_barrier_semaphore()
    count = 0
    for axis, size in axes:
        major, minor, groups = split_index(axis, size)
        peers = [2 * major + 1 - minor]
        peers += [2 * lax.rem(major + k, groups) + minor for k in range(1, groups)]
        for peer in peers:
            pl.semaphore_signal(barrier, inc=1, device_id={axis: peer}, device_id_type=MESH)
        count += len(peers)
    pl.semaphore_wait(barrier, count)


def near_first(groups):
    return sorted(range(1, groups), key=lambda k: min(k, groups - k))


def dot(a, b, ca, cb):
    return lax.dot_general(a, b, (((ca,), (cb,)), ((), ())), preferred_element_type=F32)


class Gather:
    def __init__(self, ranks, src, out, part, send, recv, local_sem):
        self.src, self.out, self.part, self.send, self.recv = src.at[part], out, part, send, recv
        self.major, self.minor, self.groups = split_index("expert", ranks)
        self.me = 2 * self.major + self.minor
        self.partner = 2 * self.major + 1 - self.minor
        self.copies = []
        self.keep = pltpu.make_async_copy(self.src, self.at(self.me), local_sem)

    def at(self, shard):
        return self.out.at[(shard, *self.part)]

    def push(self, src, shard, slot, peer):
        copy = pltpu.make_async_remote_copy(
            src_ref=src, dst_ref=self.at(shard), send_sem=self.send.at[slot], recv_sem=self.recv.at[shard],
            device_id={"expert": peer}, device_id_type=MESH,
        )
        copy.start()
        return copy

    def arrived(self, shard):
        pltpu.make_async_remote_copy(
            src_ref=self.at(shard), dst_ref=self.at(shard), send_sem=self.send.at[0],
            recv_sem=self.recv.at[shard], device_id={"expert": self.partner}, device_id_type=MESH,
        ).wait_recv()

    def start(self):
        self.keep.start()
        self.copies.append(self.push(self.src, self.me, 0, self.partner))
        for k in near_first(self.groups):
            peer = 2 * lax.rem(self.major + k, self.groups) + self.minor
            self.copies.append(self.push(self.src, self.me, k, peer))

    def sent(self):
        for copy in self.copies:
            copy.wait_send()
        self.copies = []

    def forward(self, k):
        shard = 2 * lax.rem(self.major - k + self.groups, self.groups) + self.minor
        self.arrived(shard)
        self.copies.append(self.push(self.at(shard), shard, self.groups + k - 1, self.partner))

    def finish(self):
        for k in range(self.groups):
            self.arrived(2 * lax.rem(self.major - k + self.groups, self.groups) + 1 - self.minor)
        self.keep.wait()


class Job:
    def __init__(self, axis, size, source, land, got, sems, window, part=slice(None)):
        self.part = part
        self.axis, self.source, self.land, self.got, self.window = axis, source, land, got, window
        self.s1, self.r1, self.s2, self.r2 = sems
        self.major, self.minor, self.groups = split_index(axis, size)
        self.partner = 2 * self.major + 1 - self.minor
        self.copies = []
        self.unsent = near_first(self.groups)[::-1] + [0]
        self.unsummed = list(self.unsent)

    def remote(self, src, dst, s, r, peer):
        return pltpu.make_async_remote_copy(
            src_ref=src, dst_ref=dst, send_sem=s, recv_sem=r, device_id={self.axis: peer}, device_id_type=MESH
        )

    def target(self, k):
        return lax.rem(self.major + k, self.groups)

    def own(self, k):
        return self.source.at[2 * self.target(k) + self.minor, self.part]

    def send_next(self):
        if self.unsent:
            k = self.unsent.pop(0)
            copy = self.remote(
                self.source.at[2 * self.target(k) + 1 - self.minor, self.part], self.land.at[k], self.s1.at[k], self.r1.at[k],
                self.partner,
            )
            copy.start()
            self.copies.append(copy)

    def exchange(self):
        for _ in range(self.window):
            self.send_next()

    def sum_next(self):
        if not self.unsummed:
            return
        k = self.unsummed.pop(0)
        self.remote(self.land.at[k], self.land.at[k], self.s1.at[k], self.r1.at[k], self.partner).wait_recv()
        if self.axis == "expert":
            self.send_next()
        if k:
            own = self.own(k)
            own[...] = (own[...].astype(F32) + self.land[k].astype(F32)).astype(BF16)
            copy = self.remote(
                own, self.got.at[k - 1], self.s2.at[k - 1], self.r2.at[k - 1], 2 * self.target(k) + self.minor
            )
            copy.start()
            self.copies.append(copy)

    def sum_ahead(self):
        for _ in range(self.groups - 1):
            self.sum_next()

    def finish(self):
        total = self.own(0)[...].astype(F32) + self.land[0].astype(F32)
        for k in range(1, self.groups):
            slot = self.got.at[k - 1]
            self.remote(slot, slot, self.s2.at[k - 1], self.r2.at[k - 1], self.partner).wait_recv()
            total = total + self.got[k - 1].astype(F32)
        return total

    def drain(self):
        for copy in self.copies:
            copy.wait_send()


def layer_kernel(ranks, groups_dp, exp_dev, cap, *refs):
    (ids_in, tok_in, cot_in, wg_in, wu_in, wd_in), refs = refs[:6], refs[6:]
    (out_o, out_t, out_g, out_u, out_d), refs = refs[:5], refs[5:]
    (ids_all, x_all, c_all, wg, wu, wd, pick, pick_w, x_rows, do_rows, eo), refs = refs[:11], refs[11:]
    (pre_g, pre_u, hid, gg, ug, wpart, land_e, got_e, land_w, got_w), refs = refs[:10], refs[10:]
    (g_send, g_recv, g_local, w_sem), refs = refs[:4], refs[4:]
    sems_e, sems_w = refs[:4], refs[4:]
    rows = tok_in.shape[0]
    span = wpart.shape[-1]
    groups = ranks // 2
    chunk = min(8, ranks) * cap
    parts = [slice(i, i + chunk) for i in range(0, ranks * cap, chunk)]

    loads = [pltpu.make_async_copy(a, b, w_sem.at[i]) for i, (a, b) in enumerate(((wg_in, wg), (wu_in, wu), (wd_in, wd)))]
    for load in loads:
        load.start()
    greet([("expert", ranks), ("dp", groups_dp)])
    half = rows // 2
    halves = (slice(0, half), slice(half, rows))

    def gather(t, src, out, part):
        return Gather(ranks, src, out, part, g_send.at[t], g_recv.at[t], g_local.at[t])

    dp_major, _, dp_groups = split_index("dp", groups_dp)
    wide = tok_in.shape[1] // 2
    later = dp_major // (dp_groups // 2)
    col_halves = [pl.ds(pl.multiple_of(c * wide, wide), wide) for c in (1 - later, later)]
    every = slice(None)
    g_ids = gather(0, ids_in, ids_all, (every, every))
    g_tok = [gather(1 + h, tok_in, x_all, (halves[h], every)) for h in range(2)]
    g_cot = [gather(3 + h, cot_in, c_all, (every, col_halves[h])) for h in range(2)]
    order = near_first(groups)
    for g in [g_ids] + g_tok:
        g.start()
    for k in order:
        g_ids.forward(k)
    g_ids.finish()

    first = lax.axis_index("expert") * exp_dev
    sub = lax.broadcasted_iota(jnp.int32, (8, rows), 0)
    earlier = (
        lax.broadcasted_iota(jnp.int32, (rows, rows), 0) < lax.broadcasted_iota(jnp.int32, (rows, rows), 1)
    ).astype(F32).astype(BF16)
    slots = lax.broadcasted_iota(jnp.int32, (cap, rows), 0).astype(F32)

    def place(b, carry):
        packed = ids_all[b]
        named, num = packed >> 9, packed & 511
        match = jnp.zeros((8, rows), F32)
        weight = jnp.zeros((8, rows), F32)
        for k in range(packed.shape[0]):
            hit = named[k : k + 1, :] == first + sub
            match = match + jnp.where(hit, 1.0, 0.0)
            weight = weight + jnp.where(hit, num[k : k + 1, :].astype(F32), 0.0)
        weight = weight / DENOM
        rank = dot(match.astype(BF16), earlier, 1, 0)
        slot = jnp.where(match > 0.0, rank, -1.0)
        for e in range(exp_dev):
            here = slot[e : e + 1, :] == slots
            pick[b, e * cap : (e + 1) * cap, :] = jnp.where(here, 1.0, 0.0).astype(BF16)
            pick_w[b, e * cap : (e + 1) * cap, :] = jnp.where(here, weight[e : e + 1, :], 0.0).astype(BF16)
        return carry

    lax.fori_loop(0, ranks, place, 0)

    def to_slots(sel, vals, into, cols):
        def one(b, carry):
            got = dot(sel[b], vals[b, :, cols], 1, 0).astype(BF16)
            for e in range(exp_dev):
                into[e, pl.ds(pl.multiple_of(b * cap, cap), cap), cols] = got[e * cap : (e + 1) * cap, :]
            return carry

        lax.fori_loop(0, ranks, one, 0)

    def from_slots(sel, vals, into):
        def one(b, carry):
            here = jnp.concatenate(
                [vals[e, pl.ds(pl.multiple_of(b * cap, cap), cap), :] for e in range(exp_dev)], axis=0
            )
            into[b] = dot(sel[b], here, 0, 0).astype(BF16)
            return carry

        lax.fori_loop(0, ranks, one, 0)

    for g, following in zip(g_tok, g_cot):
        for k in order:
            g.forward(k)
        following.start()
    for g in g_tok:
        g.finish()
    to_slots(pick, x_all, x_rows, every)
    for load in loads:
        load.wait()
    ahead = [(g, k) for g in g_cot for k in order]

    def forward_next():
        if ahead:
            g, k = ahead.pop(0)
            g.forward(k)

    for e in range(exp_dev):
        for part in parts:
            xr = x_rows[e, part, :]
            gate = dot(xr, wg[e], 1, 0)
            up = dot(xr, wu[e], 1, 0)
            pre_g[e, part, :] = gate
            pre_u[e, part, :] = up
            hid[e, part, :] = (gate * jax.nn.sigmoid(gate) * up).astype(BF16)
        forward_next()
        for part in parts:
            eo[e, part, :] = dot(hid[e, part, :], wd[e], 1, 0).astype(BF16)
        forward_next()
    while ahead:
        forward_next()
    for g in g_tok:
        g.sent()
    jobs_o, jobs_t = [
        [
            Job("expert", ranks, whole, land_e.at[j, h], got_e.at[j, h], [s.at[j, h] for s in sems_e], 1, halves[h])
            for h in range(2)
        ]
        for j, whole in enumerate((x_all, c_all))
    ]
    w_jobs = [
        Job("dp", groups_dp, wpart.at[j, e], land_w.at[j, e], got_w.at[j, e], [s.at[j, e] for s in sems_w], window)
        for e in range(exp_dev)
        for j, window in ((0, groups_dp), (1, groups_dp), (2, dp_groups - 1))
    ]

    def weight_block(j, e, left, right, i):
        cols = pl.ds(pl.multiple_of(i * span, span), span)
        wpart[j, e, i] = dot(left, right[e, :, cols], 0, 0).astype(BF16)

    def down_half(h):
        g_cot[h].finish()
        to_slots(pick_w, c_all, do_rows, col_halves[h])
        for e in range(exp_dev):
            for n in range(dp_groups):
                weight_block(2, e, hid[e], do_rows, (later if h else 1 - later) * dp_groups + n)
            if h == 0 and dp_groups == 2:
                w_jobs[3 * e + 2].exchange()

    down_half(0)
    from_slots(pick_w, eo, x_all)
    for job in jobs_o:
        job.exchange()
    if dp_groups == 2:
        for e in range(exp_dev):
            w_jobs[3 * e + 2].sum_ahead()
    down_half(1)
    for e in range(exp_dev):
        if dp_groups != 2:
            w_jobs[3 * e + 2].exchange()
        w_jobs[3 * e + 2].send_next()
    for e in range(exp_dev):
        mine = w_jobs[3 * e : 3 * e + 3]

        def weight_part(j, left, right):
            for i in range(groups_dp):
                weight_block(j, e, left, right, i)
            mine[j].exchange()

        for part in parts:
            gate, up = pre_g[e, part, :], pre_u[e, part, :]
            hidden_grad = dot(do_rows[e, part, :], wd[e], 1, 1)
            sig = jax.nn.sigmoid(gate)
            gg[part, :] = (hidden_grad * up * sig * (1.0 + gate * (1.0 - sig))).astype(BF16)
            ug[part, :] = (hidden_grad * (gate * sig)).astype(BF16)
        if dp_groups != 2:
            mine[2].sum_ahead()
        weight_part(0, gg[...], x_rows)
        weight_part(1, ug[...], x_rows)
        mine[0].sum_ahead()
        for part in parts:
            eo[e, part, :] = (dot(gg[part, :], wg[e], 1, 1) + dot(ug[part, :], wu[e], 1, 1)).astype(BF16)
        mine[1].sum_ahead()
        for job in jobs_o:
            job.sum_next()
    for g in g_cot:
        g.sent()
    from_slots(pick, eo, c_all)
    for job in jobs_t:
        job.exchange()
    for jobs in (jobs_o, jobs_t):
        for _ in range(groups):
            for job in jobs:
                job.sum_next()
    for job in w_jobs:
        job.sum_next()
    for n, job in enumerate(w_jobs):
        total = job.finish()
        if n % 3 == 2:
            out_d[n // 3] = total.astype(BF16)
        else:
            (out_g, out_u)[n % 3][n // 3] = total.T.astype(BF16)
    for jobs, out in ((jobs_o, out_o), (jobs_t, out_t)):
        for job in jobs:
            out[job.part, :] = job.finish().astype(BF16)
    for job in jobs_o + jobs_t + w_jobs:
        job.drain()
    g_ids.sent()


def copy_kernel(*refs):
    copies = [pltpu.make_async_copy(a, b, refs[10].at[i]) for i, (a, b) in enumerate(zip(refs[:5], refs[5:10]))]
    for copy in copies:
        copy.start()
    for copy in copies:
        copy.wait()


def local(tokens, expert_ids, route_num, w_gate, w_up, w_down, cotangent):
    ranks, groups_dp = lax.axis_size("expert"), lax.axis_size("dp")
    exp_dev, width, ff = w_gate.shape
    rows = tokens.shape[0]
    capacity = 5 * rows // 16
    cap = -(-capacity // 16) * 16
    span = width // groups_dp
    m_e, m_d = ranks // 2, groups_dp // 2
    packed = (expert_ids * 512 + route_num).T

    def sems(lead, groups):
        return [pltpu.SemaphoreType.DMA((*lead, groups)) for _ in range(4)]

    grad = jax.ShapeDtypeStruct((exp_dev, span, ff), BF16)
    out_shape = [jax.ShapeDtypeStruct((rows, width), BF16)] * 2 + [grad] * 2
    out_shape += [jax.ShapeDtypeStruct((exp_dev, ff, span), BF16)]
    results = pl.pallas_call(
        functools.partial(layer_kernel, ranks, groups_dp, exp_dev, cap),
        out_shape=out_shape,
        in_specs=[ANY] * 6,
        out_specs=[VMEM] * 5,
        scratch_shapes=[
            pltpu.VMEM((ranks, *packed.shape), jnp.int32),
            pltpu.VMEM((ranks, rows, width), BF16),
            pltpu.VMEM((ranks, rows, width), BF16),
            pltpu.VMEM(w_gate.shape, BF16),
            pltpu.VMEM(w_up.shape, BF16),
            pltpu.VMEM(w_down.shape, BF16),
            pltpu.VMEM((ranks, exp_dev * cap, rows), BF16),
            pltpu.VMEM((ranks, exp_dev * cap, rows), BF16),
            pltpu.VMEM((exp_dev, ranks * cap, width), BF16),
            pltpu.VMEM((exp_dev, ranks * cap, width), BF16),
            pltpu.VMEM((exp_dev, ranks * cap, width), BF16),
            pltpu.VMEM((exp_dev, ranks * cap, ff), F32),
            pltpu.VMEM((exp_dev, ranks * cap, ff), F32),
            pltpu.VMEM((exp_dev, ranks * cap, ff), BF16),
            pltpu.VMEM((ranks * cap, ff), BF16),
            pltpu.VMEM((ranks * cap, ff), BF16),
            pltpu.VMEM((3, exp_dev, groups_dp, ff, span), BF16),
            pltpu.VMEM((2, 2, m_e, rows // 2, width), BF16),
            pltpu.VMEM((2, 2, m_e - 1, rows // 2, width), BF16),
            pltpu.VMEM((3, exp_dev, m_d, ff, span), BF16),
            pltpu.VMEM((3, exp_dev, m_d - 1, ff, span), BF16),
            pltpu.SemaphoreType.DMA((5, ranks)),
            pltpu.SemaphoreType.DMA((5, ranks)),
            pltpu.SemaphoreType.DMA((5,)),
            pltpu.SemaphoreType.DMA((3,)),
            *sems((2, 2), m_e),
            *sems((3, exp_dev), m_d),
        ],
        compiler_params=pltpu.CompilerParams(
            collective_id=0, has_side_effects=True, vmem_limit_bytes=60 * 1024 * 1024
        ),
    )(packed, tokens, cotangent, w_gate, w_up, w_down)
    return tuple(pl.pallas_call(
        copy_kernel, out_shape=out_shape, in_specs=[ANY] * 5, out_specs=[VMEM] * 5,
        scratch_shapes=[pltpu.SemaphoreType.DMA((5,))],
        compiler_params=pltpu.CompilerParams(vmem_limit_bytes=60 * 1024 * 1024),
    )(*results))


def solution(mesh):
    in_specs = (
        P(("dp", "expert"), None),
        P(("dp", "expert"), None),
        P(("dp", "expert"), None),
        P("expert", None, None),
        P("expert", None, None),
        P("expert", None, None),
        P(("dp", "expert"), None),
    )
    out_specs = (
        P(("dp", "expert"), None),
        P(("dp", "expert"), None),
        P("expert", "dp", None),
        P("expert", "dp", None),
        P("expert", None, "dp"),
    )
    return jax.shard_map(local, mesh=mesh, in_specs=in_specs, out_specs=out_specs, check_vma=False)
```
